32 devices in a mesh: groups: 2 (over y), gx: 4 (over x, core), gy: 4 (over z).
Axes of the slice: x: 2, y: 2, z: 4, core: 2. Of those that a mesh axis runs over, the one named last changes fastest.
Arguments:
- activations: bfloat16 [128, 8192], P(('groups', 'gy'), 'gx'), parts along dimension 0, may hold values from -6 to 6
- gate_quant: bfloat16 [8192, 30720], P('gx', 'gy'), may hold values from -0.0625 to 0.0625
- gate_scale: float32 [64, 240], P('gx', 'gy'), may hold values from 0.3 to 3
- up_quant: bfloat16 [8192, 30720], P('gx', 'gy'), may hold values from -0.0625 to 0.0625
- up_scale: float32 [64, 240], P('gx', 'gy'), may hold values from 0.3 to 3
- down_quant: bfloat16 [30720, 8192], P('gy', 'gx'), may hold values from -0.03125 to 0.03125
- down_scale: float32 [240, 64], P('gy', 'gx'), may hold values from 0.3 to 3
Outputs:
- ffn_out: bfloat16 [128, 8192], P(('groups', 'gy'), 'gx'), parts along dimension 0
The draws below stay inside these ranges and needn't reach their ends.
There are 2 independent parts, one for each index of `groups`. The reference program is written for one: setup_inputs(seed, part) draws one part's arguments, and reference() takes and returns one part's arrays. A program takes and returns all parts, laid end to end along the dimension named above; an argument that names none is the same for every part. Nothing has to cross between parts.
All inputs are finite; a program needn't handle non-finite values.
Results may differ from the reference program's by a relative error of at most 0.0071.
Values may be sent and summed in bfloat16 or wider, within the bound.
No kernel may reach another device: no remote copies, remote signals or barrier semaphores. Data moves between devices by JAX's collectives and lax.ppermute only.
A program may use at most 256 MiB of HBM per device.

```python
import math
import jax
import jax.numpy as jnp

D = 8192
FF = 30720
BLOCK = 128
ROWS = 64


def block_scale(rng, extent, pieces, least, high):
    gain, own = 1.0, jax.random.fold_in(rng, 6)
    for axis_at, blocks in pieces:
        steps = jnp.exp(jax.random.uniform(jax.random.fold_in(own, axis_at), (blocks,), jnp.float32, least / len(pieces), high / len(pieces)))
        gain = gain * jnp.repeat(steps, extent[axis_at] // blocks).reshape([-1 if axis == axis_at else 1 for axis in range(len(extent))])
    return gain


def gaussian(key, shape, deviation, limit, pieces=(), dtype=jnp.bfloat16):
    values = jax.random.normal(key, shape, jnp.float32) * deviation
    if len(pieces) > 0:
        values = block_scale(key, shape, pieces, -0.22, 0.18) * values
    return jnp.clip(values, min=-limit, max=limit).astype(dtype)


def setup_inputs(seed: int = 0, part: int = 0) -> dict:
    arg_keys = jax.random.split(jax.random.key(seed), 8)
    part_splits = jax.random.split(jax.random.fold_in(arg_keys[7], part), 8)
    return {
        "activations": gaussian(part_splits[0], (ROWS, D), 1.0, 6.0, ((0, 4), (1, 4))),
        "gate_quant": gaussian(arg_keys[1], (D, FF), D ** -0.5, 0.0625, ((0, 4), (1, 4))),
        "gate_scale": jnp.clip(jnp.exp(math.log(3.0) - 2.3025851 * jax.random.uniform(arg_keys[2], (D // BLOCK, FF // BLOCK), jnp.float32) ** block_scale(arg_keys[2], (D // BLOCK, FF // BLOCK), ((0, 4), (1, 4)), -0.2, 0.2)), 0.3, 3.0),
        "up_quant": gaussian(arg_keys[3], (D, FF), D ** -0.5, 0.0625, ((0, 4), (1, 4))),
        "up_scale": jnp.clip(jnp.exp(math.log(3.0) - 2.3025851 * jax.random.uniform(arg_keys[4], (D // BLOCK, FF // BLOCK), jnp.float32) ** block_scale(arg_keys[4], (D // BLOCK, FF // BLOCK), ((0, 4), (1, 4)), -0.2, 0.2)), 0.3, 3.0),
        "down_quant": gaussian(arg_keys[5], (FF, D), FF ** -0.5, 0.03125, ((0, 4), (1, 4))),
        "down_scale": jnp.clip(jnp.exp(math.log(3.0) - 2.3025851 * jax.random.uniform(arg_keys[6], (FF // BLOCK, D // BLOCK), jnp.float32) ** block_scale(arg_keys[6], (FF // BLOCK, D // BLOCK), ((0, 4), (1, 4)), -0.2, 0.2)), 0.3, 3.0),
    }


def dequantize(quant, scales):
    rows_count = quant.shape[0]
    columns = quant.shape[1]
    spread = jnp.repeat(scales.astype(jnp.float32), BLOCK, axis=1)
    blocked = quant.reshape(rows_count // BLOCK, BLOCK, columns)
    scaled = blocked.astype(jnp.float32) * spread[:, None, :]
    return scaled.astype(jnp.bfloat16).reshape(rows_count, columns)


def reference(activations, gate_quant, gate_scale, up_quant, up_scale, down_quant, down_scale):
    gate_weight = dequantize(gate_quant, gate_scale)
    gate = jnp.dot(activations, gate_weight, preferred_element_type=jnp.float32)
    up_weight = dequantize(up_quant, up_scale)
    up_values = jnp.dot(activations, up_weight, preferred_element_type=jnp.float32)
    hidden = (jax.nn.silu(gate) * up_values).astype(jnp.bfloat16)
    down_weight = dequantize(down_quant, down_scale)
    return jnp.dot(hidden, down_weight, preferred_element_type=jnp.float32).astype(jnp.bfloat16)
```

```python
import functools

import jax
import jax.numpy as jnp
from jax import lax
from jax.experimental import pallas as pl
from jax.experimental.pallas import tpu as pltpu
from jax.sharding import PartitionSpec as P

BLOCK = 128
SPLIT = (0.4, 0.4, 0.2)
VMEM_LIMIT = 40 * 2**20


def bits_of(count):
    return count.bit_length() - 1


def reverse_bits(value, count):
    out = 0
    for _ in range(bits_of(count)):
        out, value = out * 2 + value % 2, value // 2
    return out


def swap(value, axis, size, step):
    return lax.ppermute(value, axis, [(i, i ^ step) for i in range(size)])


def chunk_sizes(blocks):
    sizes, done = [], 0
    for at in range(len(SPLIT)):
        upto = blocks if at == len(SPLIT) - 1 else round(blocks * sum(SPLIT[: at + 1]))
        sizes.append(upto - done)
        done = upto
    return [size for size in sizes if size > 0]


def load_rows(gx, refs, xs, wide):
    me = lax.axis_index("gx")
    per = refs[0].shape[0]
    sub = per * len(refs) // gx
    target = xs if sub % 16 == 0 else wide
    for slot in range(gx):
        for block in range(gx):

            @pl.when(me == block ^ reverse_bits(slot, gx))
            def _():
                first = block * sub
                if sub % per == 0:
                    for i in range(sub // per):
                        target[slot * sub + i * per : slot * sub + (i + 1) * per, :] = refs[first // per + i][...].astype(target.dtype)
                else:
                    value = refs[first // per][...].astype(target.dtype)
                    target[slot * sub : (slot + 1) * sub, :] = value[first % per : first % per + sub, :]

    if target is wide:
        xs[...] = wide[...].astype(xs.dtype)


def add_blocks(acc, xs, w, scale, row0, col0, depth):
    width = w.shape[1]

    def one(k, first):
        rows = pl.ds(pl.multiple_of(k * BLOCK, BLOCK), BLOCK)
        part = jnp.dot(xs[:, rows], w[rows, :], preferred_element_type=jnp.float32)
        pieces = [
            part[:, c * BLOCK : (c + 1) * BLOCK] * scale[row0 + k, col0 + c]
            for c in range(width // BLOCK)
        ]
        part = jnp.concatenate(pieces, axis=1)
        acc[...] = acc[...] + part

    for i in range(depth[1]):
        one(depth[0] + i, False)


def piece_blocks(blocks):
    return 2 if blocks % 2 == 0 else 1


def gate_up_kernel(gx, gy, block0, *refs):
    rows = refs[:gy]
    gate_q, up_q, gate_s, up_s, keep, send, xs, wide, gate_w, up_w, gate, up, sems = refs[gy:]
    blocks = gate_w.shape[0] // BLOCK
    width = gate_w.shape[1]
    step = piece_blocks(blocks)
    deep = step * BLOCK

    def copies(p):
        at = pl.ds(pl.multiple_of(p * deep, deep), deep)
        cols = pl.ds(block0 * BLOCK, width)
        return (
            pltpu.make_async_copy(gate_q.at[at, cols], gate_w.at[at, :], sems.at[0, p]),
            pltpu.make_async_copy(up_q.at[at, cols], up_w.at[at, :], sems.at[1, p]),
        )

    for p in range(blocks // step):
        for copy in copies(p):
            copy.start()
    load_rows(gx, rows, xs, wide)
    gate[...] = jnp.zeros_like(gate)
    up[...] = jnp.zeros_like(up)

    def body(p, carry):
        first, second = copies(p)
        first.wait()
        add_blocks(gate, xs, gate_w, gate_s, 0, block0, (p * step, step))
        second.wait()
        add_blocks(up, xs, up_w, up_s, 0, block0, (p * step, step))
        return carry

    lax.fori_loop(0, blocks // step, body, 0)
    half = keep.shape[0]
    keep[:, :width] = gate[:half, :]
    keep[:, width:] = up[:half, :]
    send[:, :width] = gate[half:, :].astype(send.dtype)
    send[:, width:] = up[half:, :].astype(send.dtype)


def gate_up(gx, gy, block0, count, rows, gate_q, up_q, gate_s, up_s):
    depth = gate_q.shape[0]
    total = rows[0].shape[0] * gy
    width = count * BLOCK
    pieces = depth // BLOCK // piece_blocks(depth // BLOCK)
    whole = pl.BlockSpec(memory_space=pltpu.VMEM)
    return pl.pallas_call(
        functools.partial(gate_up_kernel, gx, gy, block0),
        out_shape=(
            jax.ShapeDtypeStruct((total // 2, 2 * width), jnp.float32),
            jax.ShapeDtypeStruct((total // 2, 2 * width), jnp.bfloat16),
        ),
        in_specs=[whole] * gy
        + [pl.BlockSpec(memory_space=pl.ANY)] * 2
        + [pl.BlockSpec(memory_space=pltpu.SMEM)] * 2,
        out_specs=(whole, whole),
        scratch_shapes=[
            pltpu.VMEM((total, depth), jnp.bfloat16),
            pltpu.VMEM((total, depth), jnp.float32),
            pltpu.VMEM((depth, width), jnp.bfloat16),
            pltpu.VMEM((depth, width), jnp.bfloat16),
            pltpu.VMEM((total, width), jnp.float32),
            pltpu.VMEM((total, width), jnp.float32),
            pltpu.SemaphoreType.DMA((2, pieces)),
        ],
        cost_estimate=pl.CostEstimate(
            flops=4 * total * depth * width, bytes_accessed=4 * depth * width, transcendentals=0
        ),
        compiler_params=pltpu.CompilerParams(vmem_limit_bytes=VMEM_LIMIT),
    )(*rows, gate_q, up_q, gate_s, up_s)


def down_kernel(gx, gy, block0, parts, last, has_prior, *refs):
    hidden = refs[:parts]
    refs = refs[parts:]
    prior = None
    if has_prior:
        prior, refs = refs[0], refs[1:]
    down_q, down_s = refs[:2]
    outs = refs[2:-4] if last else refs[2:3]
    xs, w, acc, sems = refs[-4:]
    blocks = w.shape[0] // BLOCK
    step = piece_blocks(blocks)
    deep = step * BLOCK

    def copy(p):
        at = pl.multiple_of(p * deep, deep)
        return pltpu.make_async_copy(
            down_q.at[pl.ds(block0 * BLOCK + at, deep), :], w.at[pl.ds(at, deep), :], sems.at[p]
        )

    for p in range(blocks // step):
        copy(p).start()
    at = 0
    for ref in hidden:
        xs[at : at + ref.shape[0], :] = ref[...].astype(xs.dtype)
        at += ref.shape[0]
    if prior is None:
        acc[...] = jnp.zeros_like(acc)
    else:
        acc[...] = prior[...]

    def body(p, carry):
        copy(p).wait()
        add_blocks(acc, xs, w, down_s, block0, 0, (p * step, step))
        return carry

    lax.fori_loop(0, blocks // step, body, 0)
    if not last:
        outs[0][...] = acc[...]
        return
    me = lax.axis_index("gx")
    per = outs[0].shape[0]
    sub = xs.shape[0] // gx
    for slot in range(gx):
        for block in range(gx):

            @pl.when(me == block ^ reverse_bits(slot, gx))
            def _():
                first = block * sub
                if sub % per == 0:
                    for i in range(sub // per):
                        out = outs[first // per + i]
                        out[...] = acc[slot * sub + i * per : slot * sub + (i + 1) * per, :].astype(out.dtype)
                else:
                    out = outs[first // per]
                    out[first % per : first % per + sub, :] = acc[slot * sub : (slot + 1) * sub, :].astype(out.dtype)


def down(gx, gy, block0, count, hidden, prior, down_q, down_s, last):
    total = sum(part.shape[0] for part in hidden)
    depth, width = count * BLOCK, down_q.shape[1]
    whole = pl.BlockSpec(memory_space=pltpu.VMEM)
    per = total // gy
    if last:
        sent = jnp.bfloat16 if per // 16 * 16 == per and total // gx % 16 == 0 else jnp.float32
        out_shape = [jax.ShapeDtypeStruct((per, width), jnp.float32 if r == 0 else sent) for r in range(gy)]
    else:
        out_shape = [jax.ShapeDtypeStruct((total, width), jnp.float32)]
    before = [] if prior is None else [prior]
    return pl.pallas_call(
        functools.partial(down_kernel, gx, gy, block0, len(hidden), last, prior is not None),
        out_shape=out_shape,
        in_specs=[whole] * (len(hidden) + len(before))
        + [pl.BlockSpec(memory_space=pl.ANY), pl.BlockSpec(memory_space=pltpu.SMEM)],
        out_specs=[whole] * len(out_shape),
        scratch_shapes=[
            pltpu.VMEM((total, depth), jnp.bfloat16),
            pltpu.VMEM((depth, width), jnp.bfloat16),
            pltpu.VMEM((total, width), jnp.float32),
            pltpu.SemaphoreType.DMA((count // piece_blocks(count),)),
        ],
        cost_estimate=pl.CostEstimate(
            flops=2 * total * depth * width, bytes_accessed=2 * depth * width, transcendentals=0
        ),
        compiler_params=pltpu.CompilerParams(vmem_limit_bytes=VMEM_LIMIT),
    )(*hidden, *before, down_q, down_s)


def reduce_and_activate(gx, keep, send):
    for step in range(bits_of(gx)):
        got = swap(send, "gx", gx, 1 << step)
        total = keep + got.astype(jnp.float32)
        if step < bits_of(gx) - 1:
            half = total.shape[0] // 2
            keep, send = total[:half], total[half:].astype(jnp.bfloat16)
    middle = total.shape[1] // 2
    return (jax.nn.silu(total[:, :middle]) * total[:, middle:]).astype(jnp.bfloat16)


def spread(gx, own):
    held = [own]
    for step in reversed(range(bits_of(gx))):
        held = held + [swap(block, "gx", gx, 1 << step) for block in held]
    return held


def body(gx, gy, activations, gate_q, gate_s, up_q, up_s, down_q, down_s):
    rows = [activations] + [swap(activations, "gy", gy, r) for r in range(1, gy)]
    counts = chunk_sizes(gate_q.shape[1] // BLOCK)
    starts = [sum(counts[:i]) for i in range(len(counts))]
    hidden = []
    for block0, count in zip(starts, counts):
        keep, send = gate_up(gx, gy, block0, count, rows, gate_q, up_q, gate_s, up_s)
        hidden.append(spread(gx, reduce_and_activate(gx, keep, send)))
    prior = None
    for i, (block0, count) in enumerate(zip(starts, counts)):
        last = i == len(counts) - 1
        outs = down(gx, gy, block0, count, hidden[i], prior, down_q, down_s, last)
        prior = outs[0]
    total = outs[0]
    for r in range(1, gy):
        total = total + swap(outs[r], "gy", gy, r).astype(jnp.float32)
    return total.astype(jnp.bfloat16)


def solution(mesh):
    placed = (
        P(("groups", "gy"), "gx"),
        P("gx", "gy"),
        P("gx", "gy"),
        P("gx", "gy"),
        P("gx", "gy"),
        P("gy", "gx"),
        P("gy", "gx"),
    )
    return jax.shard_map(
        functools.partial(body, mesh.shape["gx"], mesh.shape["gy"]),
        mesh=mesh,
        in_specs=placed,
        out_specs=P(("groups", "gy"), "gx"),
        check_vma=False,
    )
```

```python
import functools

import jax
import jax.numpy as jnp
from jax import lax
from jax.experimental import pallas as pl
from jax.experimental.pallas import tpu as pltpu
from jax.sharding import PartitionSpec as P

BLOCK = 128
STRIP = 6
UNITS = 5
VMEM_LIMIT = 4 * 2**20
DOWN = 2
HEAD = ("g0a", "g0b", "u0a", "u0b", "g1a", "g1b")
STEPS = (
    ("up", 0, ("u1a", "u1b", "g2a")),
    ("fetch", 0, ("g2b",)),
    ("join", 0, ()),
    ("up", 1, ("u2a", "u2b", "g3a")),
    ("fetch", 0, ("g3b",)),
    ("act", 0, ()),
    ("join", 1, ()),
    ("up", 2, ("u3a", "u3b", "g4a")),
    ("fetch", 0, ("g4b",)),
    ("act", 1, ()),
    ("join", 2, ()),
    ("up", 3, ("u4a", "u4b", "d0a")),
    ("fetch", 0, ("d0b",)),
    ("act", 2, ()),
    ("join", 3, ()),
    ("up", 4, ("d1a", "d1b", "d2a")),
    ("fetch", 0, ("d2b",)),
    ("act", 3, ()),
    ("join", 4, ()),
    ("down", 0, ("d3a", "d3b")),
    ("down", 1, ("d4a", "d4b")),
    ("act", 4, ()),
    ("down", 2, ()),
    ("down", 3, ()),
    ("last", 4, ()),
)

IN_HBM = pl.BlockSpec(memory_space=pltpu.HBM)
IN_VMEM = pl.BlockSpec(memory_space=pltpu.VMEM)
ANYWHERE = pl.BlockSpec(memory_space=pl.ANY)


def swap(value, axis, size, step):
    return lax.ppermute(value, axis, [(i, i ^ step) for i in range(size)])


def shaped(shape, dtype):
    return jax.ShapeDtypeStruct(shape, dtype)


def strip_of(blocks):
    return max(d for d in range(1, STRIP + 1) if blocks % d == 0)


def split_refs(refs, *counts):
    out, at = [], 0
    for count in counts:
        out.append(refs[at : at + count])
        at += count
    return out


def call(kernel, operands, outs, scratch, flops, read):
    specs, arrays = zip(*operands)
    return pl.pallas_call(
        kernel,
        out_shape=outs,
        in_specs=specs,
        out_specs=[IN_VMEM] * len(outs),
        scratch_shapes=scratch,
        cost_estimate=pl.CostEstimate(flops=flops, bytes_accessed=read, transcendentals=0),
        compiler_params=pltpu.CompilerParams(vmem_limit_bytes=VMEM_LIMIT),
    )(*arrays)


class Fetch:
    def __init__(self, plan):
        self.plan = plan

    def shapes(self):
        return [shaped(piece[3], jnp.bfloat16) for piece in self.plan]

    def bytes(self):
        return sum(2 * piece[3][0] * piece[3][1] for piece in self.plan)

    def sems(self):
        return pltpu.SemaphoreType.DMA((max(len(self.plan), 1),))

    def copies(self, sources, outs, sems):
        return [
            pltpu.make_async_copy(
                sources[which].at[pl.ds(row * BLOCK, shape[0]), pl.ds(col * BLOCK, shape[1])], out, sems.at[i]
            )
            for i, ((which, row, col, shape), out) in enumerate(zip(self.plan, outs))
        ]


def fetch_only(weights, fetch, after):
    def kernel(*refs):
        sources, _, outs, (sems,) = split_refs(refs, 3, len(after), len(fetch.plan), 1)
        copies = fetch.copies(sources, outs, sems)
        for copy in copies:
            copy.start()
        for copy in copies:
            copy.wait()

    return call(
        kernel,
        [(IN_HBM, a) for a in weights] + [(ANYWHERE, a) for a in after],
        fetch.shapes(),
        [fetch.sems()],
        0,
        fetch.bytes(),
    )


def spread_columns(scale, out):
    for c in range(scale.shape[1]):
        out[:, c * BLOCK : (c + 1) * BLOCK] = jnp.broadcast_to(scale[:, c : c + 1], (scale.shape[0], BLOCK))


def head(own, scales, down_scale, weights, fetch):
    count = len(scales)

    def kernel(*refs):
        (own_ref, *scale_refs), (down_ref,), sources, (own_out, *spread), (down_out,), outs, small, (sems, own_sems) = split_refs(
            refs, 1 + count, 1, 3, 1 + count, 1, len(fetch.plan), 1 + count, 2
        )
        copies = [
            pltpu.make_async_copy(ref, to, own_sems.at[i])
            for i, (ref, to) in enumerate(zip([*scale_refs, down_ref, own_ref], [*small, own_out]))
        ]
        copies += fetch.copies(sources, outs, sems)
        for copy in copies:
            copy.start()
        for copy in copies[: 2 + count]:
            copy.wait()
        for ref, out in zip(small[:count], spread):
            spread_columns(ref[...], out)
        spread_columns(jnp.transpose(small[count][...]), down_out)
        for copy in copies[2 + count :]:
            copy.wait()

    operands = [own, *scales, down_scale.T, *weights]
    outs = call(
        kernel,
        [(IN_HBM, pltpu.with_memory_space_constraint(a, pltpu.HBM)) for a in operands],
        [shaped(own.shape, own.dtype)]
        + [shaped((s.shape[0], s.shape[1] * BLOCK), jnp.float32) for s in [*scales, down_scale]]
        + fetch.shapes(),
        [pltpu.VMEM(s.shape, jnp.float32) for s in [*scales, down_scale.T]]
        + [fetch.sems(), pltpu.SemaphoreType.DMA((2 + count,))],
        0,
        fetch.bytes(),
    )
    return outs[0], outs[1 : 2 + count], outs[2 + count :]


def scaled_product(xs, weights, scale, row0, columns, scale_columns):
    total, k = None, 0
    for w in weights:
        for i in range(w.shape[0] // BLOCK):
            part = jnp.dot(
                xs[:, k * BLOCK : (k + 1) * BLOCK],
                w[i * BLOCK : (i + 1) * BLOCK, columns],
                preferred_element_type=jnp.float32,
            )
            part = part * scale[row0 + k : row0 + k + 1, scale_columns]
            total = part if total is None else total + part
            k += 1
    return total


def gate_up(rows, block0, gates, ups, scales, weights, fetch, after):
    ordered = len(rows) == 1
    depth, total = rows[0].shape[1], sum(r.shape[0] for r in rows)
    width = gates[0].shape[1]
    parts = len(gates)
    half = width // 2
    extra = 0 if ordered else 1
    strip = strip_of(half // BLOCK)
    per = half // BLOCK // strip

    def kernel(*refs):
        row_refs, gate_w, up_w, (gate_s, up_s), sources, _, (keep, send), xs_out, outs, (sems,) = split_refs(
            refs, len(rows), parts, parts, 2, 3, len(after), 2, extra, len(fetch.plan), 1
        )
        copies = fetch.copies(sources, outs, sems)
        for copy in copies:
            copy.start()
        xs = row_refs[0]
        if not ordered:
            xs = xs_out[0]
            at = 0
            for ref in row_refs:
                xs[at : at + ref.shape[0], :] = ref[...]
                at += ref.shape[0]
        core = lax.rem(lax.axis_index("gx"), 2)

        def body(step, carry):
            slot, within = step // per, lax.rem(step, per)
            first = lax.rem(slot + core, 2) * (half // BLOCK) + within * strip
            columns = pl.ds(pl.multiple_of(first * BLOCK, BLOCK), strip * BLOCK)
            for which, (w, s) in enumerate(((gate_w, gate_s), (up_w, up_s))):
                scale_columns = pl.ds(pl.multiple_of((block0 + first) * BLOCK, BLOCK), strip * BLOCK)
                value = scaled_product(xs, w, s, 0, columns, scale_columns)
                at = pl.ds(pl.multiple_of(which * half + within * strip * BLOCK, BLOCK), strip * BLOCK)

                @pl.when(slot == 0)
                def _():
                    keep[:, at] = value

                @pl.when(slot == 1)
                def _():
                    send[:, at] = value.astype(send.dtype)

            return carry

        lax.fori_loop(0, 2 * per, body, 0)
        for copy in copies:
            copy.wait()

    outs = call(
        kernel,
        [(IN_VMEM, a) for a in [*rows, *gates, *ups, *scales]]
        + [(IN_HBM, a) for a in weights]
        + [(ANYWHERE, a) for a in after],
        [shaped((total, width), jnp.float32), shaped((total, width), jnp.bfloat16)]
        + [shaped((total, depth), jnp.bfloat16)] * extra
        + fetch.shapes(),
        [fetch.sems()],
        4 * total * depth * width,
        4 * depth * width + fetch.bytes(),
    )
    return outs[0], outs[1], outs[2 : 2 + extra], outs[2 + extra :]


def by_strips(blocks, work):
    strip = strip_of(blocks)

    def body(step, carry):
        work(pl.multiple_of(step * strip * BLOCK, BLOCK), strip * BLOCK)
        return carry

    lax.fori_loop(0, blocks // strip, body, 0)


def join(keep, got, after):
    rows, width = keep.shape

    def kernel(keep_ref, got_ref, *rest):
        total_ref, send_ref = rest[len(after) :]

        def work(left, size):
            at = pl.ds(left, size)
            total = keep_ref[:, at] + got_ref[:, at].astype(jnp.float32)
            total_ref[:, at] = total
            send_ref[:, at] = total.astype(send_ref.dtype)

        by_strips(width // BLOCK, work)

    return call(
        kernel,
        [(IN_VMEM, keep), (IN_VMEM, got)] + [(ANYWHERE, a) for a in after],
        [shaped((rows, width), jnp.float32), shaped((rows, width), jnp.bfloat16)],
        [],
        rows * width,
        12 * rows * width,
    )


def activate(keep, got, after):
    rows, middle = keep.shape[0], keep.shape[1] // 2

    def kernel(keep_ref, got_ref, *rest):
        out = rest[-1]

        def work(left, size):
            gate_at, up_at = pl.ds(left, size), pl.ds(pl.multiple_of(middle + left, BLOCK), size)
            gate = keep_ref[:, gate_at] + got_ref[:, gate_at].astype(jnp.float32)
            up = keep_ref[:, up_at] + got_ref[:, up_at].astype(jnp.float32)
            out[:, gate_at] = (jax.nn.silu(gate) * up).astype(out.dtype)

        by_strips(middle // BLOCK, work)

    return call(
        kernel,
        [(IN_VMEM, keep), (IN_VMEM, got)] + [(ANYWHERE, a) for a in after],
        [shaped((rows, middle), jnp.bfloat16)],
        [],
        8 * rows * middle,
        14 * rows * middle,
    )[0]


def down(gy, own, other, prior, block0, units, scale, weights, fetch, after, last):
    total, half = own.shape
    depth, width = sum(u.shape[0] for u in units), units[0].shape[1]
    per = total // gy
    if last:
        result = [shaped((per, width), jnp.float32 if r == 0 else jnp.bfloat16) for r in range(gy)]
    else:
        result = [shaped((total, width), jnp.float32)]
    before = [] if prior is None else [prior]
    strip = strip_of(width // BLOCK)

    def kernel(*refs):
        (own_ref, other_ref), befores, w, (scale_ref,), sources, _, results, outs, (xs, sems) = split_refs(
            refs, 2, len(before), len(units), 1, 3, len(after), len(result), len(fetch.plan), 2
        )
        copies = fetch.copies(sources, outs, sems)
        for copy in copies:
            copy.start()
        core = lax.rem(lax.axis_index("gx"), 2)
        for slot, ref in enumerate((own_ref, other_ref)):
            xs[:, pl.ds(pl.multiple_of(lax.rem(core + slot, 2) * half, BLOCK), half)] = ref[...]

        def body(step, carry):
            columns = pl.ds(pl.multiple_of(step * strip * BLOCK, BLOCK), strip * BLOCK)
            value = scaled_product(xs, w, scale_ref, block0, columns, columns)
            if befores:
                value = value + befores[0][:, columns]
            if last:
                for r, out in enumerate(results):
                    out[:, columns] = value[r * per : (r + 1) * per].astype(out.dtype)
            else:
                results[0][:, columns] = value
            return carry

        lax.fori_loop(0, width // BLOCK // strip, body, 0)
        for copy in copies:
            copy.wait()

    outs = call(
        kernel,
        [(IN_VMEM, a) for a in [own, other, *before, *units, scale]]
        + [(IN_HBM, a) for a in weights]
        + [(ANYWHERE, a) for a in after],
        result + fetch.shapes(),
        [pltpu.VMEM((total, depth), jnp.bfloat16), fetch.sems()],
        2 * total * depth * width,
        2 * depth * width + fetch.bytes(),
    )
    return outs[: len(result)], outs[len(result) :]


def body(gx, gy, activations, gate_q, gate_s, up_q, up_s, down_q, down_s):
    weights = tuple(pltpu.with_memory_space_constraint(w, pltpu.HBM) for w in (gate_q, up_q, down_q))
    depth, width = gate_q.shape[0], down_q.shape[1]
    blocks = gate_q.shape[1] // BLOCK
    at = [2 * round(blocks / 2 * i / UNITS) for i in range(UNITS + 1)]
    later = [1 << k for k in range(1, gx.bit_length() - 1)]

    def planned(names):
        out = []
        for name in names:
            kind, unit, part = "gud".index(name[0]), int(name[1:-1]), "ab".index(name[-1])
            first, count = at[unit], at[unit + 1] - at[unit]
            if kind == DOWN:
                cut = count // 2
                first, count = (first, cut) if part == 0 else (first + cut, count - cut)
                out.append((kind, first, 0, (count * BLOCK, width)))
            else:
                cut = depth // BLOCK // 2
                low, high = (0, cut) if part == 0 else (cut, depth // BLOCK)
                out.append((kind, low, first, ((high - low) * BLOCK, count * BLOCK)))
        return Fetch(out)

    def pieces(letter, unit):
        return [held[f"{letter}{unit}{part}"] for part in "ab"]

    rows = [activations] + [swap(activations, "gy", gy, r) for r in range(1, gy)]
    rows[0], (*scales, down_s), arrays = head(activations, (gate_s, up_s), down_s, weights, planned(HEAD))
    held = dict(zip(HEAD, arrays))

    sums, hidden, total, after = {}, {}, None, []
    for op, unit, names in STEPS:
        arrays = []
        if op == "up":
            keep, send, ordered, arrays = gate_up(
                rows, at[unit], pieces("g", unit), pieces("u", unit), scales, weights, planned(names), after
            )
            rows = list(ordered) or rows
            sums[unit] = (keep, swap(send, "gx", gx, 1))
            after = [keep]
        elif op == "join":
            for step in later:
                keep, send = join(*sums[unit], after)
                sums[unit] = (keep, swap(send, "gx", gx, step))
                after = [keep]
        elif op == "act":
            own = activate(*sums[unit], after)
            hidden[unit] = (own, swap(own, "gx", gx, 1))
            after = [own]
        elif op == "fetch":
            arrays = fetch_only(weights, planned(names), after)
            after = [arrays[0]]
        else:
            outs, arrays = down(
                gy,
                *hidden[unit],
                total,
                at[unit],
                pieces("d", unit),
                down_s,
                weights,
                planned(names),
                after,
                op == "last",
            )
            total = outs[0]
            after = [total]
        held.update(zip(names, arrays))
    for r in range(1, gy):
        total = total + swap(outs[r], "gy", gy, r).astype(jnp.float32)
    return total.astype(jnp.bfloat16)


def solution(mesh):
    placed = (
        P(("groups", "gy"), "gx"),
        P("gx", "gy"),
        P("gx", "gy"),
        P("gx", "gy"),
        P("gx", "gy"),
        P("gy", "gx"),
        P("gy", "gx"),
    )
    return jax.shard_map(
        functools.partial(body, mesh.shape["gx"], mesh.shape["gy"]),
        mesh=mesh,
        in_specs=placed,
        out_specs=P(("groups", "gy"), "gx"),
        check_vma=False,
    )
```

```python
import functools

import jax
import jax.numpy as jnp
from jax import lax
from jax.experimental import pallas as pl
from jax.experimental.pallas import tpu as pltpu
from jax.sharding import PartitionSpec as P

BLOCK = 128
STRIP = 8
VMEM_LIMIT = 4 * 2**20
DOWN = 2
SPLIT = (24, 20, 16)
PARTS = 8
HEAD = 268
STEPS = (
    ("up", 0, 165),
    ("fetch", 0, 60),
    ("join", 0, 0),
    ("up", 1, 150),
    ("fetch", 0, 65),
    ("join", 1, 0),
    ("act", 0, 0),
    ("up", 2, 100),
    ("fetch", 0, 60),
    ("join", 2, 0),
    ("act", 1, 0),
    ("down", 0, 70),
    ("down", 1, 70),
    ("act", 2, 0),
    ("last", 2, 0),
)

IN_HBM = pl.BlockSpec(memory_space=pltpu.HBM)
IN_VMEM = pl.BlockSpec(memory_space=pltpu.VMEM)
ANYWHERE = pl.BlockSpec(memory_space=pl.ANY)


def swap(value, axis, size, step):
    return lax.ppermute(value, axis, [(i, i ^ step) for i in range(size)])


def shaped(shape, dtype):
    return jax.ShapeDtypeStruct(shape, dtype)


def strip_of(blocks):
    return max(d for d in range(1, STRIP + 1) if blocks % d == 0)


def split_refs(refs, *counts):
    out, at = [], 0
    for count in counts:
        out.append(refs[at : at + count])
        at += count
    return out


def call(kernel, operands, outs, scratch, flops, read):
    specs, arrays = zip(*operands)
    return pl.pallas_call(
        kernel,
        out_shape=outs,
        in_specs=specs,
        out_specs=[IN_VMEM] * len(outs),
        scratch_shapes=scratch,
        cost_estimate=pl.CostEstimate(flops=flops, bytes_accessed=read, transcendentals=0),
        compiler_params=pltpu.CompilerParams(vmem_limit_bytes=VMEM_LIMIT),
    )(*arrays)


class Fetch:
    def __init__(self, plan):
        self.plan = plan

    def shapes(self):
        return [shaped(piece[3], jnp.bfloat16) for piece in self.plan]

    def bytes(self):
        return sum(2 * piece[3][0] * piece[3][1] for piece in self.plan)

    def sems(self):
        return pltpu.SemaphoreType.DMA((max(len(self.plan), 1),))

    def copies(self, sources, outs, sems):
        return [
            pltpu.make_async_copy(
                sources[which].at[pl.ds(row * BLOCK, shape[0]), pl.ds(col * BLOCK, shape[1])], out, sems.at[i]
            )
            for i, ((which, row, col, shape), out) in enumerate(zip(self.plan, outs))
        ]


def fetch_only(weights, fetch, after):
    def kernel(*refs):
        sources, _, outs, (sems,) = split_refs(refs, 3, len(after), len(fetch.plan), 1)
        copies = fetch.copies(sources, outs, sems)
        for copy in copies:
            copy.start()
        for copy in copies:
            copy.wait()

    return call(
        kernel,
        [(IN_HBM, a) for a in weights] + [(ANYWHERE, a) for a in after],
        fetch.shapes(),
        [fetch.sems()],
        0,
        fetch.bytes(),
    )


def spread_columns(scale, out):
    for c in range(scale.shape[1]):
        out[:, c * BLOCK : (c + 1) * BLOCK] = jnp.broadcast_to(scale[:, c : c + 1], (scale.shape[0], BLOCK))


def head(own, scales, down_scale, weights, fetch):
    count = len(scales)

    def kernel(*refs):
        (own_ref, *scale_refs), (down_ref,), sources, (own_out, *spread), (down_out,), outs, small, (sems, own_sems) = split_refs(
            refs, 1 + count, 1, 3, 1 + count, 1, len(fetch.plan), 1 + count, 2
        )
        copies = [
            pltpu.make_async_copy(ref, to, own_sems.at[i])
            for i, (ref, to) in enumerate(zip([*scale_refs, down_ref, own_ref], [*small, own_out]))
        ]
        copies += fetch.copies(sources, outs, sems)
        for copy in copies:
            copy.start()
        for copy in copies[: 2 + count]:
            copy.wait()
        for ref, out in zip(small[:count], spread):
            spread_columns(ref[...], out)
        spread_columns(jnp.transpose(small[count][...]), down_out)
        for copy in copies[2 + count :]:
            copy.wait()

    operands = [own, *scales, down_scale.T, *weights]
    outs = call(
        kernel,
        [(IN_HBM, pltpu.with_memory_space_constraint(a, pltpu.HBM)) for a in operands],
        [shaped(own.shape, own.dtype)]
        + [shaped((s.shape[0], s.shape[1] * BLOCK), jnp.float32) for s in [*scales, down_scale]]
        + fetch.shapes(),
        [pltpu.VMEM(s.shape, jnp.float32) for s in [*scales, down_scale.T]]
        + [fetch.sems(), pltpu.SemaphoreType.DMA((2 + count,))],
        0,
        fetch.bytes(),
    )
    return outs[0], outs[1 : 2 + count], outs[2 + count :]


def scaled_product(xs, weights, scale, row0, columns, scale_columns):
    total, k = None, 0
    for w in weights:
        for i in range(w.shape[0] // BLOCK):
            part = jnp.dot(
                xs[:, k * BLOCK : (k + 1) * BLOCK],
                w[i * BLOCK : (i + 1) * BLOCK, columns],
                preferred_element_type=jnp.float32,
            )
            part = part * scale[row0 + k : row0 + k + 1, scale_columns]
            total = part if total is None else total + part
            k += 1
    return total


def gate_up(rows, block0, gates, ups, scales, weights, fetch, after):
    ordered = len(rows) == 1
    depth, total = rows[0].shape[1], sum(r.shape[0] for r in rows)
    width = gates[0].shape[1]
    parts = len(gates)
    half = width // 2
    extra = 0 if ordered else 1
    strip = strip_of(half // BLOCK)
    per = half // BLOCK // strip

    def kernel(*refs):
        row_refs, gate_w, up_w, (gate_s, up_s), sources, _, (keep, send), xs_out, outs, (sems,) = split_refs(
            refs, len(rows), parts, parts, 2, 3, len(after), 2, extra, len(fetch.plan), 1
        )
        copies = fetch.copies(sources, outs, sems)
        for copy in copies:
            copy.start()
        xs = row_refs[0]
        if not ordered:
            xs = xs_out[0]
            at = 0
            for ref in row_refs:
                xs[at : at + ref.shape[0], :] = ref[...]
                at += ref.shape[0]
        core = lax.rem(lax.axis_index("gx"), 2)

        def body(step, carry):
            slot, within = step // per, lax.rem(step, per)
            first = lax.rem(slot + core, 2) * (half // BLOCK) + within * strip
            columns = pl.ds(pl.multiple_of(first * BLOCK, BLOCK), strip * BLOCK)
            for which, (w, s) in enumerate(((gate_w, gate_s), (up_w, up_s))):
                scale_columns = pl.ds(pl.multiple_of((block0 + first) * BLOCK, BLOCK), strip * BLOCK)
                value = scaled_product(xs, w, s, 0, columns, scale_columns)
                at = pl.ds(pl.multiple_of(which * half + within * strip * BLOCK, BLOCK), strip * BLOCK)

                @pl.when(slot == 0)
                def _():
                    keep[:, at] = value

                @pl.when(slot == 1)
                def _():
                    send[:, at] = value.astype(send.dtype)

            return carry

        lax.fori_loop(0, 2 * per, body, 0)
        for copy in copies:
            copy.wait()

    outs = call(
        kernel,
        [(IN_VMEM, a) for a in [*rows, *gates, *ups, *scales]]
        + [(IN_HBM, a) for a in weights]
        + [(ANYWHERE, a) for a in after],
        [shaped((total, width), jnp.float32), shaped((total, width), jnp.bfloat16)]
        + [shaped((total, depth), jnp.bfloat16)] * extra
        + fetch.shapes(),
        [fetch.sems()],
        4 * total * depth * width,
        4 * depth * width + fetch.bytes(),
    )
    return outs[0], outs[1], outs[2 : 2 + extra], outs[2 + extra :]


def by_strips(blocks, work):
    strip = strip_of(blocks)

    def body(step, carry):
        work(pl.multiple_of(step * strip * BLOCK, BLOCK), strip * BLOCK)
        return carry

    lax.fori_loop(0, blocks // strip, body, 0)


def join(keep, got, after):
    rows, width = keep.shape

    def kernel(keep_ref, got_ref, *rest):
        total_ref, send_ref = rest[len(after) :]

        def work(left, size):
            at = pl.ds(left, size)
            total = keep_ref[:, at] + got_ref[:, at].astype(jnp.float32)
            total_ref[:, at] = total
            send_ref[:, at] = total.astype(send_ref.dtype)

        by_strips(width // BLOCK, work)

    return call(
        kernel,
        [(IN_VMEM, keep), (IN_VMEM, got)] + [(ANYWHERE, a) for a in after],
        [shaped((rows, width), jnp.float32), shaped((rows, width), jnp.bfloat16)],
        [],
        rows * width,
        12 * rows * width,
    )


def activate(keep, got, after):
    rows, middle = keep.shape[0], keep.shape[1] // 2

    def kernel(keep_ref, got_ref, *rest):
        out = rest[-1]

        def work(left, size):
            gate_at, up_at = pl.ds(left, size), pl.ds(pl.multiple_of(middle + left, BLOCK), size)
            gate = keep_ref[:, gate_at] + got_ref[:, gate_at].astype(jnp.float32)
            up = keep_ref[:, up_at] + got_ref[:, up_at].astype(jnp.float32)
            out[:, gate_at] = (jax.nn.silu(gate) * up).astype(out.dtype)

        by_strips(middle // BLOCK, work)

    return call(
        kernel,
        [(IN_VMEM, keep), (IN_VMEM, got)] + [(ANYWHERE, a) for a in after],
        [shaped((rows, middle), jnp.bfloat16)],
        [],
        8 * rows * middle,
        14 * rows * middle,
    )[0]


def down(gy, own, other, prior, block0, units, scale, weights, fetch, after, last):
    total, half = own.shape
    depth, width = sum(u.shape[0] for u in units), units[0].shape[1]
    per = total // gy
    if last:
        result = [shaped((per, width), jnp.float32 if r == 0 else jnp.bfloat16) for r in range(gy)]
    else:
        result = [shaped((total, width), jnp.float32)]
    before = [] if prior is None else [prior]
    strip = strip_of(width // BLOCK)

    def kernel(*refs):
        (own_ref, other_ref), befores, w, (scale_ref,), sources, _, results, outs, (xs, sems) = split_refs(
            refs, 2, len(before), len(units), 1, 3, len(after), len(result), len(fetch.plan), 2
        )
        copies = fetch.copies(sources, outs, sems)
        for copy in copies:
            copy.start()
        core = lax.rem(lax.axis_index("gx"), 2)
        for slot, ref in enumerate((own_ref, other_ref)):
            xs[:, pl.ds(pl.multiple_of(lax.rem(core + slot, 2) * half, BLOCK), half)] = ref[...]

        def body(step, carry):
            columns = pl.ds(pl.multiple_of(step * strip * BLOCK, BLOCK), strip * BLOCK)
            value = scaled_product(xs, w, scale_ref, block0, columns, columns)
            if befores:
                value = value + befores[0][:, columns]
            if last:
                for r, out in enumerate(results):
                    out[:, columns] = value[r * per : (r + 1) * per].astype(out.dtype)
            else:
                results[0][:, columns] = value
            return carry

        lax.fori_loop(0, width // BLOCK // strip, body, 0)
        for copy in copies:
            copy.wait()

    outs = call(
        kernel,
        [(IN_VMEM, a) for a in [own, other, *before, *units, scale]]
        + [(IN_HBM, a) for a in weights]
        + [(ANYWHERE, a) for a in after],
        result + fetch.shapes(),
        [pltpu.VMEM((total, depth), jnp.bfloat16), fetch.sems()],
        2 * total * depth * width,
        2 * depth * width + fetch.bytes(),
    )
    return outs[: len(result)], outs[len(result) :]


def body(gx, gy, activations, gate_q, gate_s, up_q, up_s, down_q, down_s):
    weights = tuple(pltpu.with_memory_space_constraint(w, pltpu.HBM) for w in (gate_q, up_q, down_q))
    depth, width = gate_q.shape[0], down_q.shape[1]
    blocks = gate_q.shape[1] // BLOCK
    at = [2 * round(blocks / 2 * sum(SPLIT[:i]) / sum(SPLIT)) for i in range(len(SPLIT) + 1)]
    later = [1 << k for k in range(1, gx.bit_length() - 1)]

    def piece_of(kind, unit, part):
        first, count = at[unit], at[unit + 1] - at[unit]
        total = count if kind == DOWN else depth // BLOCK
        low, high = total * part // PARTS, total * (part + 1) // PARTS
        if kind == DOWN:
            return kind, first + low, 0, ((high - low) * BLOCK, width)
        return kind, low, first, ((high - low) * BLOCK, count * BLOCK)

    pieces = range(len(SPLIT))
    queue = [(kind, unit, part) for unit in pieces for part in range(PARTS) for kind in (0, 1)]
    queue += [(DOWN, unit, part) for unit in pieces for part in range(PARTS)]
    queue = [(name, piece_of(*name)) for name in queue]
    queue = [item for item in queue if item[1][3][0] > 0]
    everything = 3 * depth * gate_q.shape[1]

    def take(share, needed=()):
        names, plan, size = [], [], 0
        while queue:
            name, piece = queue[0]
            size += piece[3][0] * piece[3][1]
            if size * 1000 > share * everything and name[:2] not in needed:
                break
            queue.pop(0)
            names.append(name)
            plan.append(piece)
        return names, Fetch(plan)

    def needed_after(step):
        for op, unit, share in STEPS[step + 1 :]:
            if op == "up":
                return ((0, unit), (1, unit))
            if op in ("down", "last"):
                return ((DOWN, unit),)
            if share:
                return ()
        return ()

    def held_pieces(kind, unit):
        return [held[kind, unit, part] for part in range(PARTS) if (kind, unit, part) in held]

    rows = [activations] + [swap(activations, "gy", gy, r) for r in range(1, gy)]
    names, fetch = take(HEAD, needed_after(-1))
    rows[0], (*scales, down_s), arrays = head(activations, (gate_s, up_s), down_s, weights, fetch)
    held = dict(zip(names, arrays))

    sums, hidden, total, after = {}, {}, None, []
    for step, (op, unit, share) in enumerate(STEPS):
        names, fetch = take(share, needed_after(step)) if share else ((), Fetch([]))
        arrays = []
        if op == "up":
            keep, send, ordered, arrays = gate_up(
                rows, at[unit], held_pieces(0, unit), held_pieces(1, unit), scales, weights, fetch, after
            )
            rows = list(ordered) or rows
            sums[unit] = (keep, swap(send, "gx", gx, 1))
            after = [keep]
        elif op == "join":
            for hop in later:
                keep, send = join(*sums[unit], after)
                sums[unit] = (keep, swap(send, "gx", gx, hop))
                after = [keep]
        elif op == "act":
            own = activate(*sums[unit], after)
            hidden[unit] = (own, swap(own, "gx", gx, 1))
            after = [own]
        elif op == "fetch":
            arrays = fetch_only(weights, fetch, after)
            after = [arrays[0]]
        else:
            outs, arrays = down(
                gy,
                *hidden[unit],
                total,
                at[unit],
                held_pieces(DOWN, unit),
                down_s,
                weights,
                fetch,
                after,
                op == "last",
            )
            total = outs[0]
            after = [total]
        held.update(zip(names, arrays))
    for r in range(1, gy):
        total = total + swap(outs[r], "gy", gy, r).astype(jnp.float32)
    return total.astype(jnp.bfloat16)


def solution(mesh):
    placed = (
        P(("groups", "gy"), "gx"),
        P("gx", "gy"),
        P("gx", "gy"),
        P("gx", "gy"),
        P("gx", "gy"),
        P("gy", "gx"),
        P("gy", "gx"),
    )
    return jax.shard_map(
        functools.partial(body, mesh.shape["gx"], mesh.shape["gy"]),
        mesh=mesh,
        in_specs=placed,
        out_specs=P(("groups", "gy"), "gx"),
        check_vma=False,
    )
```

```python
import functools

import jax
import jax.numpy as jnp
from jax import lax
from jax.experimental import pallas as pl
from jax.experimental.pallas import tpu as pltpu
from jax.sharding import PartitionSpec as P

BLOCK = 128
STRIP = 12
VMEM_LIMIT = 4 * 2**20
DOWN = 2
SPLIT = (24, 20, 16)
PARTS = 8
HEAD = 268
STEPS = (
    ("up", 0, 165),
    ("fetch", 0, 60),
    ("join", 0, 0),
    ("up", 1, 135),
    ("fetch", 0, 90),
    ("join", 1, 0),
    ("act", 0, 0),
    ("up", 2, 90),
    ("fetch", 0, 55),
    ("join", 2, 0),
    ("act", 1, 0),
    ("down", 0, 70),
    ("down", 1, 60),
    ("act", 2, 0),
    ("own", 2, 0),
    ("last", 2, 0),
)

IN_HBM = pl.BlockSpec(memory_space=pltpu.HBM)
IN_VMEM = pl.BlockSpec(memory_space=pltpu.VMEM)
ANYWHERE = pl.BlockSpec(memory_space=pl.ANY)


def swap(value, axis, size, step):
    return lax.ppermute(value, axis, [(i, i ^ step) for i in range(size)])


def shaped(shape, dtype):
    return jax.ShapeDtypeStruct(shape, dtype)


def strip_of(blocks):
    return max(d for d in range(1, STRIP + 1) if blocks % d == 0)


def split_refs(refs, *counts):
    out, at = [], 0
    for count in counts:
        out.append(refs[at : at + count])
        at += count
    return out


def call(kernel, operands, outs, scratch, flops, read):
    specs, arrays = zip(*operands)
    return pl.pallas_call(
        kernel,
        out_shape=outs,
        in_specs=specs,
        out_specs=[IN_VMEM] * len(outs),
        scratch_shapes=scratch,
        cost_estimate=pl.CostEstimate(flops=flops, bytes_accessed=read, transcendentals=0),
        compiler_params=pltpu.CompilerParams(vmem_limit_bytes=VMEM_LIMIT),
    )(*arrays)


class Fetch:
    def __init__(self, plan):
        self.plan = plan

    def shapes(self):
        return [shaped(piece[3], jnp.bfloat16) for piece in self.plan]

    def bytes(self):
        return sum(2 * piece[3][0] * piece[3][1] for piece in self.plan)

    def sems(self):
        return pltpu.SemaphoreType.DMA((max(len(self.plan), 1),))

    def copies(self, sources, outs, sems):
        return [
            pltpu.make_async_copy(
                sources[which].at[pl.ds(row * BLOCK, shape[0]), pl.ds(col * BLOCK, shape[1])], out, sems.at[i]
            )
            for i, ((which, row, col, shape), out) in enumerate(zip(self.plan, outs))
        ]


def fetch_only(weights, fetch, after):
    def kernel(*refs):
        sources, _, outs, (sems,) = split_refs(refs, 3, len(after), len(fetch.plan), 1)
        copies = fetch.copies(sources, outs, sems)
        for copy in copies:
            copy.start()
        for copy in copies:
            copy.wait()

    return call(
        kernel,
        [(IN_HBM, a) for a in weights] + [(ANYWHERE, a) for a in after],
        fetch.shapes(),
        [fetch.sems()],
        0,
        fetch.bytes(),
    )


def spread_columns(scale, out):
    for c in range(scale.shape[1]):
        out[:, c * BLOCK : (c + 1) * BLOCK] = jnp.broadcast_to(scale[:, c : c + 1], (scale.shape[0], BLOCK))


def head(own, scales, down_scale, weights, fetch):
    count = len(scales)

    def kernel(*refs):
        (own_ref, *scale_refs), (down_ref,), sources, (own_out, *spread), (down_out,), outs, small, (sems, own_sems) = split_refs(
            refs, 1 + count, 1, 3, 1 + count, 1, len(fetch.plan), 1 + count, 2
        )
        copies = [
            pltpu.make_async_copy(ref, to, own_sems.at[i])
            for i, (ref, to) in enumerate(zip([*scale_refs, down_ref, own_ref], [*small, own_out]))
        ]
        copies += fetch.copies(sources, outs, sems)
        for copy in copies:
            copy.start()
        for copy in copies[: 2 + count]:
            copy.wait()
        for ref, out in zip(small[:count], spread):
            spread_columns(ref[...], out)
        spread_columns(jnp.transpose(small[count][...]), down_out)
        for copy in copies[2 + count :]:
            copy.wait()

    operands = [own, *scales, down_scale.T, *weights]
    outs = call(
        kernel,
        [(IN_HBM, pltpu.with_memory_space_constraint(a, pltpu.HBM)) for a in operands],
        [shaped(own.shape, own.dtype)]
        + [shaped((s.shape[0], s.shape[1] * BLOCK), jnp.float32) for s in [*scales, down_scale]]
        + fetch.shapes(),
        [pltpu.VMEM(s.shape, jnp.float32) for s in [*scales, down_scale.T]]
        + [fetch.sems(), pltpu.SemaphoreType.DMA((2 + count,))],
        0,
        fetch.bytes(),
    )
    return outs[0], outs[1 : 2 + count], outs[2 + count :]


def scaled_product(xs, weights, scale, row0, columns, scale_columns):
    total, k = None, 0
    for w in weights:
        for i in range(w.shape[0] // BLOCK):
            part = jnp.dot(
                xs[:, k * BLOCK : (k + 1) * BLOCK],
                w[i * BLOCK : (i + 1) * BLOCK, columns],
                preferred_element_type=jnp.float32,
            )
            part = part * scale[row0 + k : row0 + k + 1, scale_columns]
            total = part if total is None else total + part
            k += 1
    return total


def gate_up(rows, block0, gates, ups, scales, weights, fetch, after):
    ordered = len(rows) == 1
    depth, total = rows[0].shape[1], sum(r.shape[0] for r in rows)
    width = gates[0].shape[1]
    parts = len(gates)
    half = width // 2
    extra = 0 if ordered else 1
    strip = strip_of(half // BLOCK)
    per = half // BLOCK // strip

    def kernel(*refs):
        row_refs, gate_w, up_w, (gate_s, up_s), sources, _, (keep, send), xs_out, outs, (sems,) = split_refs(
            refs, len(rows), parts, parts, 2, 3, len(after), 2, extra, len(fetch.plan), 1
        )
        copies = fetch.copies(sources, outs, sems)
        for copy in copies:
            copy.start()
        xs = row_refs[0]
        if not ordered:
            xs = xs_out[0]
            at = 0
            for ref in row_refs:
                xs[at : at + ref.shape[0], :] = ref[...]
                at += ref.shape[0]
        core = lax.rem(lax.axis_index("gx"), 2)

        def body(step, carry):
            slot, within = step // per, lax.rem(step, per)
            first = lax.rem(slot + core, 2) * (half // BLOCK) + within * strip
            columns = pl.ds(pl.multiple_of(first * BLOCK, BLOCK), strip * BLOCK)
            for which, (w, s) in enumerate(((gate_w, gate_s), (up_w, up_s))):
                scale_columns = pl.ds(pl.multiple_of((block0 + first) * BLOCK, BLOCK), strip * BLOCK)
                value = scaled_product(xs, w, s, 0, columns, scale_columns)
                at = pl.ds(pl.multiple_of(which * half + within * strip * BLOCK, BLOCK), strip * BLOCK)

                @pl.when(slot == 0)
                def _():
                    keep[:, at] = value

                @pl.when(slot == 1)
                def _():
                    send[:, at] = value.astype(send.dtype)

            return carry

        lax.fori_loop(0, 2 * per, body, 0)
        for copy in copies:
            copy.wait()

    outs = call(
        kernel,
        [(IN_VMEM, a) for a in [*rows, *gates, *ups, *scales]]
        + [(IN_HBM, a) for a in weights]
        + [(ANYWHERE, a) for a in after],
        [shaped((total, width), jnp.float32), shaped((total, width), jnp.bfloat16)]
        + [shaped((total, depth), jnp.bfloat16)] * extra
        + fetch.shapes(),
        [fetch.sems()],
        4 * total * depth * width,
        4 * depth * width + fetch.bytes(),
    )
    return outs[0], outs[1], outs[2 : 2 + extra], outs[2 + extra :]


def by_strips(blocks, work):
    strip = strip_of(blocks)

    def body(step, carry):
        work(pl.multiple_of(step * strip * BLOCK, BLOCK), strip * BLOCK)
        return carry

    lax.fori_loop(0, blocks // strip, body, 0)


def join(keep, got, after):
    rows, width = keep.shape

    def kernel(keep_ref, got_ref, *rest):
        total_ref, send_ref = rest[len(after) :]

        def work(left, size):
            at = pl.ds(left, size)
            total = keep_ref[:, at] + got_ref[:, at].astype(jnp.float32)
            total_ref[:, at] = total
            send_ref[:, at] = total.astype(send_ref.dtype)

        by_strips(width // BLOCK, work)

    return call(
        kernel,
        [(IN_VMEM, keep), (IN_VMEM, got)] + [(ANYWHERE, a) for a in after],
        [shaped((rows, width), jnp.float32), shaped((rows, width), jnp.bfloat16)],
        [],
        rows * width,
        12 * rows * width,
    )


def activate(keep, got, after):
    rows, middle = keep.shape[0], keep.shape[1] // 2

    def kernel(keep_ref, got_ref, *rest):
        out = rest[-1]

        def work(left, size):
            gate_at, up_at = pl.ds(left, size), pl.ds(pl.multiple_of(middle + left, BLOCK), size)
            gate = keep_ref[:, gate_at] + got_ref[:, gate_at].astype(jnp.float32)
            up = keep_ref[:, up_at] + got_ref[:, up_at].astype(jnp.float32)
            out[:, gate_at] = (jax.nn.silu(gate) * up).astype(out.dtype)

        by_strips(middle // BLOCK, work)

    return call(
        kernel,
        [(IN_VMEM, keep), (IN_VMEM, got)] + [(ANYWHERE, a) for a in after],
        [shaped((rows, middle), jnp.bfloat16)],
        [],
        8 * rows * middle,
        14 * rows * middle,
    )[0]


def down(gy, own, other, prior, block0, units, scale, weights, fetch, after, last, only=None):
    total, half = own.shape
    depth, width = sum(u.shape[0] for u in units), units[0].shape[1]
    per = total // gy
    if last:
        result = [shaped((per, width), jnp.float32 if r == 0 else jnp.bfloat16) for r in range(gy)]
    else:
        result = [shaped((total, width), jnp.float32)]
    before = [] if prior is None else [prior]
    strip = strip_of(width // BLOCK)

    def kernel(*refs):
        (own_ref, other_ref), befores, w, (scale_ref,), sources, _, results, outs, (xs, sems) = split_refs(
            refs, 2, len(before), len(units), 1, 3, len(after), len(result), len(fetch.plan), 2
        )
        copies = fetch.copies(sources, outs, sems)
        for copy in copies:
            copy.start()
        core = lax.rem(lax.axis_index("gx"), 2)

        def body(x, held_w, row0, step, carry):
            columns = pl.ds(pl.multiple_of(step * strip * BLOCK, BLOCK), strip * BLOCK)
            value = scaled_product(x, held_w, scale_ref, row0, columns, columns)
            if befores:
                value = value + befores[0][:, columns]
            if last:
                for r, out in enumerate(results):
                    out[:, columns] = value[r * per : (r + 1) * per].astype(out.dtype)
            else:
                results[0][:, columns] = value
            return carry

        def run(*operands):
            lax.fori_loop(0, width // BLOCK // strip, functools.partial(body, *operands), 0)

        if only is None:
            for slot, ref in enumerate((own_ref, other_ref)):
                xs[:, pl.ds(pl.multiple_of(lax.rem(core + slot, 2) * half, BLOCK), half)] = ref[...]
            run(xs, w, block0)
        else:
            x, parts, rows = (own_ref, other_ref)[only], ([], []), 0
            for ref in w:
                parts[rows // half].append(ref)
                rows += ref.shape[0]
            for which in (0, 1):

                @pl.when(core == (which + only) % 2)
                def _():
                    run(x, parts[which], block0 + which * half // BLOCK)

        for copy in copies:
            copy.wait()

    outs = call(
        kernel,
        [(IN_VMEM, a) for a in [own, other, *before, *units, scale]]
        + [(IN_HBM, a) for a in weights]
        + [(ANYWHERE, a) for a in after],
        result + fetch.shapes(),
        [pltpu.VMEM((total, depth), jnp.bfloat16), fetch.sems()],
        2 * total * depth * width,
        2 * depth * width + fetch.bytes(),
    )
    return outs[: len(result)], outs[len(result) :]


def body(gx, gy, activations, gate_q, gate_s, up_q, up_s, down_q, down_s):
    weights = tuple(pltpu.with_memory_space_constraint(w, pltpu.HBM) for w in (gate_q, up_q, down_q))
    depth, width = gate_q.shape[0], down_q.shape[1]
    blocks = gate_q.shape[1] // BLOCK
    at = [2 * round(blocks / 2 * sum(SPLIT[:i]) / sum(SPLIT)) for i in range(len(SPLIT) + 1)]
    later = [1 << k for k in range(1, gx.bit_length() - 1)]

    def piece_of(kind, unit, part):
        first, count = at[unit], at[unit + 1] - at[unit]
        total = count if kind == DOWN else depth // BLOCK
        low, high = total * part // PARTS, total * (part + 1) // PARTS
        if kind == DOWN:
            return kind, first + low, 0, ((high - low) * BLOCK, width)
        return kind, low, first, ((high - low) * BLOCK, count * BLOCK)

    pieces = range(len(SPLIT))
    queue = [(kind, unit, part) for unit in pieces for part in range(PARTS) for kind in (0, 1)]
    queue += [(DOWN, unit, part) for unit in pieces for part in range(PARTS)]
    queue = [(name, piece_of(*name)) for name in queue]
    queue = [item for item in queue if item[1][3][0] > 0]
    everything = 3 * depth * gate_q.shape[1]

    def take(share, needed=()):
        names, plan, size = [], [], 0
        while queue:
            name, piece = queue[0]
            size += piece[3][0] * piece[3][1]
            if names and size * 1000 > share * everything and name[:2] not in needed:
                break
            queue.pop(0)
            names.append(name)
            plan.append(piece)
        return names, Fetch(plan)

    def needed_after(step):
        for op, unit, share in STEPS[step + 1 :]:
            if op == "up":
                return ((0, unit), (1, unit))
            if op in ("down", "own", "last"):
                return ((DOWN, unit),)
            if share:
                return ()
        return ()

    def held_pieces(kind, unit):
        return [held[kind, unit, part] for part in range(PARTS) if (kind, unit, part) in held]

    rows = [activations] + [swap(activations, "gy", gy, r) for r in range(1, gy)]
    names, fetch = take(HEAD, needed_after(-1))
    rows[0], (*scales, down_s), arrays = head(activations, (gate_s, up_s), down_s, weights, fetch)
    held = dict(zip(names, arrays))

    sums, hidden, total, after = {}, {}, None, []
    for step, (op, unit, share) in enumerate(STEPS):
        names, fetch = take(share, needed_after(step)) if share else ((), Fetch([]))
        arrays = []
        if op == "up":
            keep, send, ordered, arrays = gate_up(
                rows, at[unit], held_pieces(0, unit), held_pieces(1, unit), scales, weights, fetch, after
            )
            rows = list(ordered) or rows
            sums[unit] = (keep, swap(send, "gx", gx, 1))
            after = [keep]
        elif op == "join":
            for hop in later:
                keep, send = join(*sums[unit], after)
                sums[unit] = (keep, swap(send, "gx", gx, hop))
                after = [keep]
        elif op == "act":
            own = activate(*sums[unit], after)
            hidden[unit] = (own, swap(own, "gx", gx, 1))
            after = [own]
        elif op == "fetch":
            arrays = fetch_only(weights, fetch, after)
            after = [arrays[0]]
        else:
            outs, arrays = down(
                gy,
                *((hidden[unit][0],) * 2 if op == "own" else hidden[unit]),
                total,
                at[unit],
                held_pieces(DOWN, unit),
                down_s,
                weights,
                fetch,
                after,
                op == "last",
                {"own": 0, "last": 1}.get(op),
            )
            total = outs[0]
            after = [total]
        held.update(zip(names, arrays))
    for r in [*range(2, gy), 1]:
        total = total + swap(outs[r], "gy", gy, r).astype(jnp.float32)
    return total.astype(jnp.bfloat16)


def solution(mesh):
    placed = (
        P(("groups", "gy"), "gx"),
        P("gx", "gy"),
        P("gx", "gy"),
        P("gx", "gy"),
        P("gx", "gy"),
        P("gy", "gx"),
        P("gy", "gx"),
    )
    return jax.shard_map(
        functools.partial(body, mesh.shape["gx"], mesh.shape["gy"]),
        mesh=mesh,
        in_specs=placed,
        out_specs=P(("groups", "gy"), "gx"),
        check_vma=False,
    )
```

```python
import functools

import jax
import jax.numpy as jnp
from jax import lax
from jax.experimental import pallas as pl
from jax.experimental.pallas import tpu as pltpu
from jax.sharding import PartitionSpec as P

BLOCK = 128
STRIP = 12
VMEM_LIMIT = 4 * 2**20
DOWN = 2
SPLIT = (24, 20, 16)
PARTS = 8
HEAD = 268
STEPS = (
    ("up", 0, 165),
    ("fetch", 0, 60),
    ("join", 0, 0),
    ("up", 1, 135),
    ("fetch", 0, 100),
    ("join", 1, 0),
    ("act", 0, 0),
    ("up", 2, 95),
    ("fetch", 0, 55),
    ("join", 2, 0),
    ("act", 1, 0),
    ("down", 0, 75),
    ("down", 1, 60),
    ("act", 2, 0),
    ("own", 2, 0),
    ("last", 2, 0),
)

IN_HBM = pl.BlockSpec(memory_space=pltpu.HBM)
IN_VMEM = pl.BlockSpec(memory_space=pltpu.VMEM)
ANYWHERE = pl.BlockSpec(memory_space=pl.ANY)


def swap(value, axis, size, step):
    return lax.ppermute(value, axis, [(i, i ^ step) for i in range(size)])


def shaped(shape, dtype):
    return jax.ShapeDtypeStruct(shape, dtype)


def strip_of(blocks):
    return max(d for d in range(1, STRIP + 1) if blocks % d == 0)


def split_refs(refs, *counts):
    out, at = [], 0
    for count in counts:
        out.append(refs[at : at + count])
        at += count
    return out


def call(kernel, operands, outs, scratch, flops, read):
    specs, arrays = zip(*operands)
    return pl.pallas_call(
        kernel,
        out_shape=outs,
        in_specs=specs,
        out_specs=[IN_VMEM] * len(outs),
        scratch_shapes=scratch,
        cost_estimate=pl.CostEstimate(flops=flops, bytes_accessed=read, transcendentals=0),
        compiler_params=pltpu.CompilerParams(vmem_limit_bytes=VMEM_LIMIT),
    )(*arrays)


class Fetch:
    def __init__(self, plan):
        self.plan = plan

    def shapes(self):
        return [shaped(piece[3], jnp.bfloat16) for piece in self.plan]

    def bytes(self):
        return sum(2 * piece[3][0] * piece[3][1] for piece in self.plan)

    def sems(self):
        return pltpu.SemaphoreType.DMA((max(len(self.plan), 1),))

    def copies(self, sources, outs, sems):
        return [
            pltpu.make_async_copy(
                sources[which].at[pl.ds(row * BLOCK, shape[0]), pl.ds(col * BLOCK, shape[1])], out, sems.at[i]
            )
            for i, ((which, row, col, shape), out) in enumerate(zip(self.plan, outs))
        ]


def fetch_only(weights, fetch, after):
    def kernel(*refs):
        sources, _, outs, (sems,) = split_refs(refs, 3, len(after), len(fetch.plan), 1)
        copies = fetch.copies(sources, outs, sems)
        for copy in copies:
            copy.start()
        for copy in copies:
            copy.wait()

    return call(
        kernel,
        [(IN_HBM, a) for a in weights] + [(ANYWHERE, a) for a in after],
        fetch.shapes(),
        [fetch.sems()],
        0,
        fetch.bytes(),
    )


def spread_columns(scale, out):
    for c in range(scale.shape[1]):
        out[:, c * BLOCK : (c + 1) * BLOCK] = jnp.broadcast_to(scale[:, c : c + 1], (scale.shape[0], BLOCK))


def head(own, scales, down_scale, weights, fetch):
    count = len(scales)

    def kernel(*refs):
        (own_ref, *scale_refs), (down_ref,), sources, (own_out, *spread), (down_out,), outs, small, (sems, own_sems) = split_refs(
            refs, 1 + count, 1, 3, 1 + count, 1, len(fetch.plan), 1 + count, 2
        )
        copies = [
            pltpu.make_async_copy(ref, to, own_sems.at[i])
            for i, (ref, to) in enumerate(zip([*scale_refs, down_ref, own_ref], [*small, own_out]))
        ]
        copies += fetch.copies(sources, outs, sems)
        for copy in copies:
            copy.start()
        for copy in copies[: 2 + count]:
            copy.wait()
        for ref, out in zip(small[:count], spread):
            spread_columns(ref[...], out)
        spread_columns(jnp.transpose(small[count][...]), down_out)
        for copy in copies[2 + count :]:
            copy.wait()

    operands = [own, *scales, down_scale.T, *weights]
    outs = call(
        kernel,
        [(IN_HBM, pltpu.with_memory_space_constraint(a, pltpu.HBM)) for a in operands],
        [shaped(own.shape, own.dtype)]
        + [shaped((s.shape[0], s.shape[1] * BLOCK), jnp.float32) for s in [*scales, down_scale]]
        + fetch.shapes(),
        [pltpu.VMEM(s.shape, jnp.float32) for s in [*scales, down_scale.T]]
        + [fetch.sems(), pltpu.SemaphoreType.DMA((2 + count,))],
        0,
        fetch.bytes(),
    )
    return outs[0], outs[1 : 2 + count], outs[2 + count :]


def scaled_product(xs, weights, scale, row0, columns, scale_columns):
    total, k = None, 0
    for w in weights:
        for i in range(w.shape[0] // BLOCK):
            part = jnp.dot(
                xs[:, k * BLOCK : (k + 1) * BLOCK],
                w[i * BLOCK : (i + 1) * BLOCK, columns],
                preferred_element_type=jnp.float32,
            )
            part = part * scale[row0 + k : row0 + k + 1, scale_columns]
            total = part if total is None else total + part
            k += 1
    return total


def gate_up(rows, block0, gates, ups, scales, weights, fetch, after):
    ordered = len(rows) == 1
    depth, total = rows[0].shape[1], sum(r.shape[0] for r in rows)
    width = gates[0].shape[1]
    parts = len(gates)
    half = width // 2
    extra = 0 if ordered else 1
    strip = strip_of(half // BLOCK)
    per = half // BLOCK // strip

    def kernel(*refs):
        row_refs, gate_w, up_w, (gate_s, up_s), sources, _, (keep, send), xs_out, outs, (sems,) = split_refs(
            refs, len(rows), parts, parts, 2, 3, len(after), 2, extra, len(fetch.plan), 1
        )
        copies = fetch.copies(sources, outs, sems)
        for copy in copies:
            copy.start()
        xs = row_refs[0]
        if not ordered:
            xs = xs_out[0]
            at = 0
            for ref in row_refs:
                xs[at : at + ref.shape[0], :] = ref[...]
                at += ref.shape[0]
        core = lax.rem(lax.axis_index("gx"), 2)

        def body(step, carry):
            slot, within = step // per, lax.rem(step, per)
            first = lax.rem(slot + core, 2) * (half // BLOCK) + within * strip
            columns = pl.ds(pl.multiple_of(first * BLOCK, BLOCK), strip * BLOCK)
            for which, (w, s) in enumerate(((gate_w, gate_s), (up_w, up_s))):
                scale_columns = pl.ds(pl.multiple_of((block0 + first) * BLOCK, BLOCK), strip * BLOCK)
                value = scaled_product(xs, w, s, 0, columns, scale_columns)
                at = pl.ds(pl.multiple_of(which * half + within * strip * BLOCK, BLOCK), strip * BLOCK)

                @pl.when(slot == 0)
                def _():
                    keep[:, at] = value

                @pl.when(slot == 1)
                def _():
                    send[:, at] = value.astype(send.dtype)

            return carry

        lax.fori_loop(0, 2 * per, body, 0)
        for copy in copies:
            copy.wait()

    outs = call(
        kernel,
        [(IN_VMEM, a) for a in [*rows, *gates, *ups, *scales]]
        + [(IN_HBM, a) for a in weights]
        + [(ANYWHERE, a) for a in after],
        [shaped((total, width), jnp.float32), shaped((total, width), jnp.bfloat16)]
        + [shaped((total, depth), jnp.bfloat16)] * extra
        + fetch.shapes(),
        [fetch.sems()],
        4 * total * depth * width,
        4 * depth * width + fetch.bytes(),
    )
    return outs[0], outs[1], outs[2 : 2 + extra], outs[2 + extra :]


def by_strips(blocks, work):
    strip = strip_of(blocks)

    def body(step, carry):
        work(pl.multiple_of(step * strip * BLOCK, BLOCK), strip * BLOCK)
        return carry

    lax.fori_loop(0, blocks // strip, body, 0)


def join(keep, got, after):
    rows, width = keep.shape

    def kernel(keep_ref, got_ref, *rest):
        total_ref, send_ref = rest[len(after) :]

        def work(left, size):
            at = pl.ds(left, size)
            total = keep_ref[:, at] + got_ref[:, at].astype(jnp.float32)
            total_ref[:, at] = total
            send_ref[:, at] = total.astype(send_ref.dtype)

        by_strips(width // BLOCK, work)

    return call(
        kernel,
        [(IN_VMEM, keep), (IN_VMEM, got)] + [(ANYWHERE, a) for a in after],
        [shaped((rows, width), jnp.float32), shaped((rows, width), jnp.bfloat16)],
        [],
        rows * width,
        12 * rows * width,
    )


def activate(keep, got, after):
    rows, middle = keep.shape[0], keep.shape[1] // 2

    def kernel(keep_ref, got_ref, *rest):
        out = rest[-1]

        def work(left, size):
            gate_at, up_at = pl.ds(left, size), pl.ds(pl.multiple_of(middle + left, BLOCK), size)
            gate = keep_ref[:, gate_at] + got_ref[:, gate_at].astype(jnp.float32)
            up = keep_ref[:, up_at] + got_ref[:, up_at].astype(jnp.float32)
            out[:, gate_at] = (jax.nn.silu(gate) * up).astype(out.dtype)

        by_strips(middle // BLOCK, work)

    return call(
        kernel,
        [(IN_VMEM, keep), (IN_VMEM, got)] + [(ANYWHERE, a) for a in after],
        [shaped((rows, middle), jnp.bfloat16)],
        [],
        8 * rows * middle,
        14 * rows * middle,
    )[0]


def down(gy, own, other, prior, block0, units, scale, weights, fetch, after, last, only=None):
    total, half = own.shape
    depth, width = sum(u.shape[0] for u in units), units[0].shape[1]
    per = total // gy
    if last:
        result = [shaped((per, width), jnp.float32 if r == 0 else jnp.bfloat16) for r in range(gy)]
    else:
        result = [shaped((total, width), jnp.float32)]
    before = [] if prior is None else [prior]
    strip = strip_of(width // BLOCK)

    def kernel(*refs):
        (own_ref, other_ref), befores, w, (scale_ref,), sources, _, results, outs, (xs, sems) = split_refs(
            refs, 2, len(before), len(units), 1, 3, len(after), len(result), len(fetch.plan), 2
        )
        copies = fetch.copies(sources, outs, sems)
        for copy in copies:
            copy.start()
        core = lax.rem(lax.axis_index("gx"), 2)

        def body(x, held_w, row0, step, carry):
            columns = pl.ds(pl.multiple_of(step * strip * BLOCK, BLOCK), strip * BLOCK)
            value = scaled_product(x, held_w, scale_ref, row0, columns, columns)
            if befores:
                value = value + befores[0][:, columns]
            if last:
                for r, out in enumerate(results):
                    out[:, columns] = value[r * per : (r + 1) * per].astype(out.dtype)
            else:
                results[0][:, columns] = value
            return carry

        def run(*operands):
            lax.fori_loop(0, width // BLOCK // strip, functools.partial(body, *operands), 0)

        if only is None:
            for slot, ref in enumerate((own_ref, other_ref)):
                xs[:, pl.ds(pl.multiple_of(lax.rem(core + slot, 2) * half, BLOCK), half)] = ref[...]
            run(xs, w, block0)
        else:
            x, parts, rows = (own_ref, other_ref)[only], ([], []), 0
            for ref in w:
                parts[rows // half].append(ref)
                rows += ref.shape[0]
            for which in (0, 1):

                @pl.when(core == (which + only) % 2)
                def _():
                    run(x, parts[which], block0 + which * half // BLOCK)

        for copy in copies:
            copy.wait()

    outs = call(
        kernel,
        [(IN_VMEM, a) for a in [own, other, *before, *units, scale]]
        + [(IN_HBM, a) for a in weights]
        + [(ANYWHERE, a) for a in after],
        result + fetch.shapes(),
        [pltpu.VMEM((total, depth), jnp.bfloat16), fetch.sems()],
        2 * total * depth * width,
        2 * depth * width + fetch.bytes(),
    )
    return outs[: len(result)], outs[len(result) :]


def body(gx, gy, activations, gate_q, gate_s, up_q, up_s, down_q, down_s):
    weights = tuple(pltpu.with_memory_space_constraint(w, pltpu.HBM) for w in (gate_q, up_q, down_q))
    depth, width = gate_q.shape[0], down_q.shape[1]
    blocks = gate_q.shape[1] // BLOCK
    at = [2 * round(blocks / 2 * sum(SPLIT[:i]) / sum(SPLIT)) for i in range(len(SPLIT) + 1)]
    later = [1 << k for k in range(1, gx.bit_length() - 1)]

    def piece_of(kind, unit, part):
        first, count = at[unit], at[unit + 1] - at[unit]
        total = count if kind == DOWN else depth // BLOCK
        low, high = total * part // PARTS, total * (part + 1) // PARTS
        if kind == DOWN:
            return kind, first + low, 0, ((high - low) * BLOCK, width)
        return kind, low, first, ((high - low) * BLOCK, count * BLOCK)

    pieces = range(len(SPLIT))
    queue = [(kind, unit, part) for unit in pieces for part in range(PARTS) for kind in (0, 1)]
    queue += [(DOWN, unit, part) for unit in pieces for part in range(PARTS)]
    queue = [(name, piece_of(*name)) for name in queue]
    queue = [item for item in queue if item[1][3][0] > 0]
    everything = 3 * depth * gate_q.shape[1]

    def take(share, needed=()):
        names, plan, size = [], [], 0
        while queue:
            name, piece = queue[0]
            size += piece[3][0] * piece[3][1]
            if names and size * 1000 > share * everything and name[:2] not in needed:
                break
            queue.pop(0)
            names.append(name)
            plan.append(piece)
        return names, Fetch(plan)

    def needed_after(step):
        for op, unit, share in STEPS[step + 1 :]:
            if op == "up":
                return ((0, unit), (1, unit))
            if op in ("down", "own", "last"):
                return ((DOWN, unit),)
            if share:
                return ()
        return ()

    def held_pieces(kind, unit):
        return [held[kind, unit, part] for part in range(PARTS) if (kind, unit, part) in held]

    rows = [activations] + [swap(activations, "gy", gy, r) for r in range(1, gy)]
    names, fetch = take(HEAD, needed_after(-1))
    rows[0], (*scales, down_s), arrays = head(activations, (gate_s, up_s), down_s, weights, fetch)
    held = dict(zip(names, arrays))

    sums, hidden, total, after = {}, {}, None, []
    for step, (op, unit, share) in enumerate(STEPS):
        names, fetch = take(share, needed_after(step)) if share else ((), Fetch([]))
        arrays = []
        if op == "up":
            keep, send, ordered, arrays = gate_up(
                rows, at[unit], held_pieces(0, unit), held_pieces(1, unit), scales, weights, fetch, after
            )
            rows = list(ordered) or rows
            sums[unit] = (keep, swap(send, "gx", gx, 1))
            after = [keep]
        elif op == "join":
            for hop in later:
                keep, send = join(*sums[unit], after)
                sums[unit] = (keep, swap(send, "gx", gx, hop))
                after = [keep]
        elif op == "act":
            own = activate(*sums[unit], after)
            hidden[unit] = (own, swap(own, "gx", gx, 1))
            after = [own]
        elif op == "fetch":
            arrays = fetch_only(weights, fetch, after)
            after = [arrays[0]]
        else:
            outs, arrays = down(
                gy,
                *((hidden[unit][0],) * 2 if op == "own" else hidden[unit]),
                total,
                at[unit],
                held_pieces(DOWN, unit),
                down_s,
                weights,
                fetch,
                after,
                op == "last",
                {"own": 0, "last": 1}.get(op),
            )
            total = outs[0]
            after = [total]
        held.update(zip(names, arrays))
    for r in [*range(2, gy), 1]:
        total = total + swap(outs[r], "gy", gy, r).astype(jnp.float32)
    return total.astype(jnp.bfloat16)


def solution(mesh):
    placed = (
        P(("groups", "gy"), "gx"),
        P("gx", "gy"),
        P("gx", "gy"),
        P("gx", "gy"),
        P("gx", "gy"),
        P("gy", "gx"),
        P("gy", "gx"),
    )
    return jax.shard_map(
        functools.partial(body, mesh.shape["gx"], mesh.shape["gy"]),
        mesh=mesh,
        in_specs=placed,
        out_specs=P(("groups", "gy"), "gx"),
        check_vma=False,
    )
```
